128 devices in a mesh: front: 4 (over y), hss: 32 (over x, z, core).
Axes of the slice: x: 4, y: 4, z: 4, core: 2. Of those that a mesh axis runs over, the one named last changes fastest.
Arguments:
- front_rows: bfloat16 [4, 19456, 19456], P('front', 'hss'), may hold values from -0.0390625 to 0.0390625
- samples: bfloat16 [4, 19456, 256], P('front', 'hss'), may hold values from -6 to 6
- child_rows: bfloat16 [4, 16384, 256], P('front', 'hss'), may hold values from -6 to 6
- child_owner: int32 [4, 16384, 1], P('front'), may hold values from 0 to 31; in each aligned block of 512 rows (0 to 511, 512 to 1023, ..., all dimensions but the last counted through in order) at most 64 rows name the same one
- child_local: int32 [4, 16384], P('front'), may hold values from 0 to 607
- leaf_skeleton: int32 [4, 32, 128], P('front'), may hold values from 0 to 607, as said below
- merge_select: int32 [4, 31, 128], P('front'), may hold values from 0 to 255, as said below
Outputs:
- parent_sample: bfloat16 [4, 19456, 256], P('front', 'hss')
- pair_sample: float32 [4, 4096, 256], P('front', 'hss')
- root_sample: float32 [4, 128, 256], P('front')
The draws below stay inside these ranges and needn't reach their ends.
Inputs may be any that keep to these rules, and one draw needn't show every extreme that they name: `child_owner`: in the rows of one device (aligned blocks of 512 rows) no owner is named more than 64 times, a bound that some block reaches. `leaf_skeleton`: the 128 entries of one leaf are distinct. `merge_select`: the 128 entries of one node are distinct.
All inputs are finite; a program needn't handle non-finite values.
Results may differ from the reference program's by a relative error of at most 0.0013.
Values may be sent and summed in bfloat16 or wider, within the bound.
No kernel may reach another device: no remote copies, remote signals or barrier semaphores. Data moves between devices by JAX's collectives and lax.ppermute only.
A program may use at most 192 MiB of HBM per device.

```python
import math
import jax
import jax.numpy as jnp
import numpy as np

ROWS = 608
SAMPLES = 256
RANK = 128
CHILD = 512
CAP = 64
LEAVES = 32
LEVELS = 5
F = 19456
FRONTS = 4


def draw_leaf_skeleton(key, part):
    key = jax.random.fold_in(key, 11)
    keys = jax.random.split(key, FRONTS * LEAVES)
    picks = jax.vmap(lambda one_key: jax.random.permutation(one_key, ROWS)[:RANK])(keys)
    return picks.reshape(FRONTS, LEAVES, RANK).astype(jnp.int32)


def draw_merge_select(key, part):
    key = jax.random.fold_in(key, 23)
    keys = jax.random.split(key, FRONTS * (LEAVES - 1))
    picks = jax.vmap(lambda one_key: jax.random.permutation(one_key, 2 * RANK)[:RANK])(keys)
    return picks.reshape(FRONTS, LEAVES - 1, RANK).astype(jnp.int32)


def place_ends(entries, rng, smallest, high):
    longest = entries.shape.index(max(entries.shape))
    spots = []
    for shift in (0, 1):
        where = [jax.random.randint(jax.random.fold_in(rng, axis), (), 0, length) for axis, length in enumerate(entries.shape)]
        where[longest] = (where[longest] + shift) % entries.shape[longest]
        spots.append(tuple(where))
    return entries.at[spots[0]].set(smallest).at[spots[1]].set(high)


def levels(key, extent, shards, low, high):
    level = 1.0
    for position, shards_of in shards:
        draws = jax.random.uniform(jax.random.fold_in(jax.random.fold_in(key, 6), position), (shards_of,), jnp.float32, low / len(shards), high / len(shards))
        level = level * jnp.repeat(jnp.exp(draws), extent[position] // shards_of).reshape((-1,) + (1,) * (len(extent) - 1 - position))
    return level


def deal_out(key, own, number, rows, count, top, limit, lean):
    sequence = jax.random.permutation(key, count)
    heavy_load, common = portions_of(count, rows * top, limit, lean, True), portions_of(count, rows * top, limit, lean, False)
    places = jnp.arange(count)

    def named(lengths, rotation):
        used = int((lengths > 0).sum())
        fixed = max(1, used // 4)
        passed = fixed + (places - fixed + rotation * (used - fixed)) % max(1, count - fixed)
        return jnp.zeros((count,), jnp.int32).at[sequence[jnp.where(places < fixed, places, passed)]].set(jnp.asarray(lengths, jnp.int32))

    lengths = jnp.where(number % 4 == 0, named(heavy_load, number // 4), named(common, number - number // 4 - 1))
    mixed = jax.random.permutation(jax.random.fold_in(own, 3), count)
    donor, sink = mixed[0:count // 2 * 2:2], mixed[1:count // 2 * 2:2]
    room = jnp.minimum(lengths[donor] - 1, limit - lengths[sink]) // 2
    room = jnp.where((donor == sequence[0]) | (sink == sequence[0]) | (lengths[sink] == 0), 0, jnp.maximum(room, 0))
    passed = jax.random.randint(jax.random.fold_in(own, 4), (count // 2,), 0, 1 << 20) % (room + 1)
    lengths = lengths.at[donor].add(-passed).at[sink].add(passed)
    members = jnp.searchsorted(jnp.cumsum(lengths), jnp.arange(rows * top), side="right").astype(jnp.int32)
    listing = members.reshape(top, rows).T
    listing = listing[jax.random.permutation(jax.random.fold_in(own, 1), rows)]
    rotation = jax.random.randint(jax.random.fold_in(own, 2), (rows, 1), 0, top)
    return jnp.take_along_axis(listing, (jnp.arange(top)[None, :] + rotation) % top, axis=1)


def portions_of(count, total, limit, skew, full):
    weights = [(1 << 20) // math.isqrt(rank ** skew) + 1 for rank in range(1, count + 1)]
    largest = limit if full else min(limit, max(-(-total // count), total * weights[0] // sum(weights)))
    least = 1 if total - largest >= count - 1 else 0
    holding, spare = [largest] + [least] * (count - 1), total - largest - least * (count - 1)
    while spare > 0:
        movable = [i for i in range(1, count) if holding[i] < largest] or [i for i in range(1, count) if holding[i] < limit]
        mass, budget = sum([weights[i] for i in movable]), spare
        for i in movable:
            more = min(limit - holding[i], max(1, budget * weights[i] // mass), spare)
            holding[i] = holding[i] + more
            spare = spare - more
    return np.array(holding)


def noise(own_key, extent, scale, limit, cuts=(), held_as=jnp.bfloat16):
    values = jax.random.normal(own_key, extent, jnp.float32) * scale
    if len(cuts) > 0:
        values = levels(own_key, extent, cuts, -0.22, 0.18) * values
    return jnp.clip(values, min=-limit, max=limit).astype(held_as)


def setup_inputs(seed: int = 0) -> dict:
    arg_keys = jax.random.split(jax.random.key(seed), 8)
    front_rows = noise(arg_keys[0], (FRONTS, F, F), F ** -0.5, 0.0390625, ((0, 4), (1, 32)))
    samples = noise(arg_keys[1], (FRONTS, F, SAMPLES), 1.0, 6.0, ((0, 4), (1, 32)))
    child_rows = noise(arg_keys[2], (FRONTS, LEAVES * CHILD, SAMPLES), 1.0, 6.0, ((0, 4), (1, 32)))
    child_owner_keys = jax.random.split(jax.random.fold_in(arg_keys[3], 1), FRONTS * (LEAVES * CHILD) // CHILD)
    child_owner_turns = jax.random.permutation(jax.random.fold_in(arg_keys[3], 3), FRONTS * (LEAVES * CHILD) // CHILD)
    child_owner = jax.vmap(lambda own, number: deal_out(jax.random.fold_in(arg_keys[3], 2), own, number, CHILD, LEAVES, 1, CAP, 2))(child_owner_keys, child_owner_turns).reshape((FRONTS, LEAVES * CHILD, 1))
    child_local = place_ends(jax.random.randint(arg_keys[4], (FRONTS, LEAVES * CHILD), 0, ROWS), jax.random.fold_in(arg_keys[4], 1), 0, ROWS - 1).astype(jnp.int32)
    leaf_skeleton = draw_leaf_skeleton(jax.random.fold_in(arg_keys[7], 71), 0)
    merge_select = draw_merge_select(jax.random.fold_in(arg_keys[7], 71), 0)
    return dict(front_rows=front_rows, samples=samples, child_rows=child_rows, child_owner=child_owner, child_local=child_local, leaf_skeleton=leaf_skeleton, merge_select=merge_select)


def level_positions(selections, leaf_total, depth):
    tracked = [jnp.arange(leaf_total * RANK, dtype=jnp.int32).reshape(leaf_total, RANK)]
    offset = 0
    for height in range(depth):
        node_total = leaf_total >> (height + 1)
        paired = tracked[-1].reshape(node_total, 2 * RANK)
        chosen = selections[offset:offset + node_total]
        tracked.append(jax.vmap(take_line)(paired, chosen))
        offset += node_total
    return tracked


def take_line(paired_line, picked):
    return jnp.take(paired_line, picked)


def take_rows(stacked_block, picked):
    return jnp.take(stacked_block, picked, axis=0)


def take_columns(stacked_block, picked):
    return jnp.take(stacked_block, picked, axis=1)


def one_front(front_block, omega, children, owners, targets, skeletons, selections):
    product = jnp.dot(front_block, omega, preferred_element_type=jnp.float32)
    hit_rows = owners * ROWS + targets
    arrivals = jnp.zeros((F, SAMPLES), jnp.float32).at[hit_rows].add(children.astype(jnp.float32))
    full_sample = product + arrivals
    global_ids = (jnp.arange(LEAVES, dtype=jnp.int32)[:, None] * ROWS + skeletons).reshape(-1)
    skeleton_rows = jnp.take(front_block, global_ids, axis=0)
    diagonal = skeleton_rows.reshape(LEAVES, RANK, LEAVES, ROWS)[jnp.arange(LEAVES), :, jnp.arange(LEAVES), :]
    own_omega = omega.reshape(LEAVES, ROWS, SAMPLES)
    removed = jnp.einsum("nkr,nrs->nks", diagonal.astype(jnp.float32), own_omega.astype(jnp.float32))
    node_sample = jnp.take(full_sample, global_ids, axis=0).reshape(LEAVES, RANK, SAMPLES) - removed
    node_rows = jnp.take(skeleton_rows, global_ids, axis=1).reshape(LEAVES, RANK, LEAVES * RANK)
    node_omega = jnp.take(omega, global_ids, axis=0).reshape(LEAVES, RANK, SAMPLES)
    tracked = level_positions(selections, LEAVES, LEVELS)
    offset = 0
    first_level = None
    for height in range(LEVELS):
        node_total = LEAVES >> (height + 1)
        where_now = tracked[height].reshape(node_total, 2, RANK)
        sample_pair = node_sample.reshape(node_total, 2, RANK, SAMPLES)
        rows_pair = node_rows.reshape(node_total, 2, RANK, LEAVES * RANK)
        omega_pair = node_omega.reshape(node_total, 2, RANK, SAMPLES)
        cross_low = jax.vmap(take_columns)(rows_pair[:, 0], where_now[:, 1])
        cross_high = jax.vmap(take_columns)(rows_pair[:, 1], where_now[:, 0])
        fix_low = jnp.einsum("nij,njs->nis", cross_low.astype(jnp.float32), omega_pair[:, 1].astype(jnp.float32))
        fix_high = jnp.einsum("nij,njs->nis", cross_high.astype(jnp.float32), omega_pair[:, 0].astype(jnp.float32))
        stacked = jnp.concatenate([sample_pair[:, 0] - fix_low, sample_pair[:, 1] - fix_high], axis=1)
        chosen = selections[offset:offset + node_total]
        node_sample = jax.vmap(take_rows)(stacked, chosen)
        node_rows = jax.vmap(take_rows)(rows_pair.reshape(node_total, 2 * RANK, LEAVES * RANK), chosen)
        node_omega = jax.vmap(take_rows)(omega_pair.reshape(node_total, 2 * RANK, SAMPLES), chosen)
        if height == 0:
            first_level = jnp.repeat(node_sample, 2, axis=0).reshape(LEAVES * RANK, SAMPLES)
        offset += node_total
    return full_sample.astype(jnp.bfloat16), first_level, node_sample[0]


def reference(front_rows, samples, child_rows, child_owner, child_local, leaf_skeleton, merge_select):
    parents = []
    pairs = []
    roots = []
    for front_index in range(FRONTS):
        parent, pair, root = one_front(front_rows[front_index], samples[front_index], child_rows[front_index],
                                       child_owner[front_index, :, 0], child_local[front_index],
                                       leaf_skeleton[front_index], merge_select[front_index])
        parents.append(parent)
        pairs.append(pair)
        roots.append(root)
    return jnp.stack(parents), jnp.stack(pairs), jnp.stack(roots)
```

```python
import jax
import jax.numpy as jnp
from jax import lax
from jax.sharding import PartitionSpec as P

ROWS = 608
SAMPLES = 256
RANK = 128
CHILD = 512
CAP = 64
BF = jnp.bfloat16
F32 = jnp.float32


def pick_index(table, position):
    return lax.dynamic_index_in_dim(table, position, 0, keepdims=False)


def iota(n):
    return jnp.arange(n, dtype=jnp.int32)


def shifted(x, axis, move):
    return lax.ppermute(x, axis, [(i, move(i)) for i in range(lax.axis_size(axis))])


def fates(selections, leaf_total, depth):
    survived = jnp.zeros((1, RANK), jnp.int32)
    root_slot = iota(RANK)[None] + 1
    for height in reversed(range(depth)):
        offset = leaf_total - (leaf_total >> height)
        node_total = leaf_total >> (height + 1)
        chosen = selections[offset : offset + node_total]
        hit = chosen[:, :, None] == iota(2 * RANK)[None, None, :]
        survived = jnp.sum(jnp.where(hit, survived[:, :, None] + 1, 0), axis=1).reshape(-1, RANK)
        root_slot = jnp.sum(jnp.where(hit, root_slot[:, :, None], 0), axis=1).reshape(-1, RANK)
    return survived, root_slot


def total_over_hss(x, side):
    core = lambda i: i ^ 1
    along_z = lambda s: lambda i: i // 8 * 8 + (i // 2 + s) % 4 * 2 + i % 2
    along_x = lambda s: lambda i: (i + 8 * s) % 32
    half = x.shape[0] // 2
    low, high = x[:half], x[half:]
    mine = jnp.where(side == 0, low, high)
    yours = jnp.where(side == 0, high, low)
    mine = mine + shifted(yours, "hss", core)
    for along in (along_z, along_x):
        mine = mine + sum([shifted(mine, "hss", along(s)) for s in (2, 1, 3)])
    other = shifted(mine, "hss", core)
    return jnp.concatenate([jnp.where(side == 0, mine, other), jnp.where(side == 0, other, mine)], axis=0)


def body(front_rows, samples, child_rows, child_owner, child_local, leaf_skeleton, merge_select):
    leaf_total = lax.axis_size("hss")
    depth = leaf_total.bit_length() - 1
    myself = lax.axis_index("hss")
    side = jnp.bitwise_and(myself, 1)
    front = front_rows[0]
    gathered = lax.all_gather(samples[0], "hss", axis=0, tiled=True)

    owners = child_owner[0, :, 0].reshape(leaf_total, CHILD)
    targets = child_local[0].reshape(leaf_total, CHILD)
    mine = pick_index(owners, myself)
    earlier = iota(CHILD)[:, None] < iota(CHILD)[None, :]
    my_slots = jnp.sum(((mine[:, None] == mine[None, :]) & earlier).astype(jnp.int32), axis=0)
    destination = mine * CAP + my_slots
    send_select = (iota(leaf_total * CAP)[:, None] == destination[None, :]).astype(BF)
    outgoing = jnp.dot(send_select, child_rows[0], preferred_element_type=F32).astype(BF)
    incoming = lax.all_to_all(
        outgoing.reshape(leaf_total, CAP, SAMPLES), "hss", split_axis=0, concat_axis=0, tiled=True
    ).reshape(leaf_total * CAP, SAMPLES)

    hits = owners == myself
    order = jnp.dot(hits.astype(BF), earlier.astype(BF), preferred_element_type=F32).astype(jnp.int32)
    placed = jnp.where(hits, order, CAP)
    slot_hits = placed[:, :, None] == iota(CAP)[None, None, :]
    slot_rows = (jnp.sum(jnp.where(slot_hits, targets[:, :, None] + 1, 0), axis=1) - 1).reshape(-1)
    selector = (iota(ROWS)[:, None] == slot_rows[None, :]).astype(BF)

    skeletons = leaf_skeleton[0]
    survived, root_slot = fates(merge_select[0], leaf_total, depth)
    my_skeleton = pick_index(skeletons, myself)
    my_root_slot = pick_index(root_slot, myself)
    root_rows = jnp.sum(jnp.where(my_root_slot[:, None] == iota(RANK)[None, :] + 1, my_skeleton[:, None] + 1, 0), axis=0) - 1
    pair_choice = pick_index(merge_select[0], jnp.right_shift(myself, 1)) - side * RANK
    pair_rows = jnp.sum(jnp.where(iota(RANK)[:, None] == pair_choice[None, :], my_skeleton[:, None] + 1, 0), axis=0) - 1
    root_pick = (root_rows[:, None] == iota(ROWS)[None, :]).astype(BF)
    pair_pick = (pair_rows[:, None] == iota(ROWS)[None, :]).astype(BF)

    marks = jnp.sum(
        jnp.where(skeletons[:, :, None] == iota(ROWS)[None, None, :], survived[:, :, None] + 1, 0), axis=1
    )
    apart = jnp.bitwise_xor(iota(leaf_total), myself)
    level = sum([(apart >= (2 << h)).astype(jnp.int32) for h in range(depth - 1)])
    root_keep = (apart != 0)[:, None] & (marks <= level[:, None])
    pair_keep = (apart != 0)[:, None] & ((apart != 1)[:, None] | (marks == 0))
    root_front = jnp.dot(root_pick, front, preferred_element_type=F32).astype(BF)
    root_front = jnp.where(root_keep.reshape(1, -1), root_front, 0)
    pair_front = jnp.dot(pair_pick, front, preferred_element_type=F32).astype(BF)
    pair_front = jnp.where(pair_keep.reshape(1, -1), pair_front, 0)
    root_arrivals = jnp.dot(
        jnp.dot(root_pick, selector, preferred_element_type=F32).astype(BF), incoming, preferred_element_type=F32
    )
    pair_arrivals = jnp.dot(
        jnp.dot(pair_pick, selector, preferred_element_type=F32).astype(BF), incoming, preferred_element_type=F32
    )
    arrivals = jnp.dot(selector, incoming, preferred_element_type=F32)
    front, gathered, root_front, pair_front, root_arrivals, pair_arrivals, arrivals = lax.optimization_barrier(
        (front, gathered, root_front, pair_front, root_arrivals, pair_arrivals, arrivals)
    )

    root = jnp.dot(root_front, gathered, preferred_element_type=F32) + root_arrivals
    root, gathered = lax.optimization_barrier((root, gathered))
    root = total_over_hss(root, side)
    parent = (jnp.dot(front, gathered, preferred_element_type=F32) + arrivals).astype(BF)
    pair = jnp.dot(pair_front, gathered, preferred_element_type=F32) + pair_arrivals
    pair = pair + shifted(pair, "hss", lambda i: i ^ 1)
    return (parent[None], pair[None], root[None])


def solution(mesh):
    in_specs = (
        P("front", "hss", None),
        P("front", "hss", None),
        P("front", "hss", None),
        P("front", None, None),
        P("front", None),
        P("front", None, None),
        P("front", None, None),
    )
    out_specs = (P("front", "hss", None), P("front", "hss", None), P("front", None, None))
    return jax.shard_map(body, mesh=mesh, in_specs=in_specs, out_specs=out_specs, check_vma=False)
```

```python
import functools

import jax
import jax.numpy as jnp
from jax import lax
from jax.experimental import pallas as pl
from jax.experimental.pallas import tpu as pltpu
from jax.sharding import PartitionSpec as P

ROWS = 608
SAMPLES = 256
RANK = 128
CHILD = 512
CAP = 64
BF = jnp.bfloat16
F32 = jnp.float32
LANES = 128
SUBLANES = 16
WINDOW = 768
PLACES = (0, 96, 64, 160)
RING = 4
TURNS = (0, 1, 3, 2)
AHEAD = 2
VMEM = 42 << 20


def pick_index(table, position):
    return lax.dynamic_index_in_dim(table, position, 0, keepdims=False)


def iota(n):
    return jnp.arange(n, dtype=jnp.int32)


def shifted(x, move):
    return lax.ppermute(x, "hss", [(i, move(i)) for i in range(lax.axis_size("hss"))])


def cores(i):
    return i ^ 1


def along_z(turn):
    return lambda i: i ^ 2 * TURNS[turn]


def along_x(turn):
    return lambda i: i ^ 8 * TURNS[turn]


def first(turn):
    return lambda i: along_x(turn)(i) if i % 2 else along_z(turn)(i)


def second(turn):
    return lambda i: along_z(turn)(i) if i % 2 else along_x(turn)(i)


def total_over_ring(x, along):
    near, far, opposite = [shifted(x, along(turn)) for turn in (1, 2, 3)]
    return (x + near) + (far + opposite)


def fate_kernel(me_ref, select_ref, skeleton_ref, slots_ref, keep_ref):
    me = me_ref[0]
    row = lax.broadcasted_iota(jnp.int32, (SUBLANES, RANK), 0)
    once = jnp.where(row == 0, 1.0, 0.0)
    carried = [jnp.where(row == 1, lax.broadcasted_iota(jnp.int32, (SUBLANES, RANK), 1) + 1, 0).astype(F32)]
    place = lax.broadcasted_iota(jnp.int32, (2 * RANK, RANK), 0)
    at = select_ref.shape[0]
    while at > 0:
        at -= len(carried)
        below = []
        for node, values in enumerate(carried):
            hit = jnp.where(place == select_ref[at + node : at + node + 1, :], 1.0, 0.0).astype(BF)
            spread = lax.dot_general((values + once).astype(BF), hit, (((1,), (1,)), ((), ())), preferred_element_type=F32)
            below += [spread[:, :RANK], spread[:, RANK:]]
        carried = below
    gone = []
    for leaf, values in enumerate(carried):
        slots_ref[leaf : leaf + 1, :] = values[1:2, :].astype(jnp.int32)
        apart = jnp.bitwise_xor(me, leaf)
        level = sum([jnp.where(apart >= (2 << h), 1, 0) for h in range(4)])
        names = skeleton_ref[leaf : leaf + 1, :]
        gone.append(jnp.where(values[0:1, :].astype(jnp.int32) >= level, names, -WINDOW))
    gone = jnp.concatenate(gone + [gone[0]] * (RANK - len(gone)), axis=0).T
    lane = lax.broadcasted_iota(jnp.int32, (RANK, WINDOW), 1)
    for leaf in range(len(carried)):
        named = jnp.where(lane - PLACES[leaf % 4] == gone[:, leaf : leaf + 1], 1.0, 0.0)
        keep = 1.0 - jnp.max(named, axis=0, keepdims=True)
        keep_ref[leaf : leaf + 1, :] = keep * jnp.where(me == leaf, 0.0, 1.0)


def fates(me, selections, skeletons):
    leaves = skeletons.shape[0]
    return pl.pallas_call(
        fate_kernel,
        in_specs=[pl.BlockSpec(memory_space=pltpu.SMEM), pl.BlockSpec(), pl.BlockSpec()],
        out_shape=[jax.ShapeDtypeStruct((leaves, RANK), jnp.int32), jax.ShapeDtypeStruct((leaves, WINDOW), F32)],
        compiler_params=pltpu.CompilerParams(vmem_limit_bytes=VMEM),
        cost_estimate=pl.CostEstimate(flops=leaves << 20, bytes_accessed=leaves << 12, transcendentals=0),
    )(me[None], selections, skeletons)


def window_tile(leaf):
    return 19 * leaf // 4 - jnp.where(leaf % 4 == 3, 1, 0)


def window_place(leaf):
    kind = leaf % 4
    return jnp.where(kind == 0, PLACES[0], jnp.where(kind == 1, PLACES[1], jnp.where(kind == 2, PLACES[2], PLACES[3])))


def leaf_of(me, whose, step, j):
    by_first = 2 * TURNS[j] + 8 * TURNS[step]
    by_second = 8 * TURNS[j] + 2 * TURNS[step]
    side = jnp.bitwise_and(me, 1)
    moved = jnp.where(side == whose, by_first, by_second)
    return jnp.bitwise_xor(jnp.bitwise_xor(me, whose), moved)


def product_kernel(units, plain, masked, added, me_ref, front, keep_ref, *refs):
    blocks, refs = refs[: units[-1][0] + 1], refs[units[-1][0] + 1 :]
    out_ref, left_buf, right_buf, sems = refs[-4:]
    leaves = [leaf_of(me_ref[0], *unit[2:]) for unit in units]

    def copies(u):
        block, row = units[u][:2]
        slot, half = u // 2, u % 2
        columns = pl.ds(pl.multiple_of(window_tile(leaves[u]) * LANES, LANES), WINDOW)
        rows = pl.ds(pl.multiple_of(half * WINDOW + window_place(leaves[u]), 32), ROWS)
        return (
            pltpu.make_async_copy(
                front.at[:, columns], left_buf.at[slot, :, pl.ds(half * WINDOW, WINDOW)], sems.at[u, 0]
            ),
            pltpu.make_async_copy(blocks[block].at[row], right_buf.at[slot, rows, :], sems.at[u, 1]),
        )

    def begin(slot):
        for u in (2 * slot, 2 * slot + 1):
            edge = (u % 2) * WINDOW
            right_buf[slot, edge : edge + PLACES[-1], :] = jnp.zeros((PLACES[-1], SAMPLES), BF)
            right_buf[slot, edge + ROWS : edge + WINDOW, :] = jnp.zeros((WINDOW - ROWS, SAMPLES), BF)
            for copy in copies(u):
                copy.start()

    slots = len(units) // 2
    for slot in range(min(AHEAD, slots)):
        begin(slot)
    for slot in range(slots):
        for u in (2 * slot, 2 * slot + 1):
            for copy in copies(u):
                copy.wait()
        if slot + AHEAD < slots:
            begin(slot + AHEAD)
        at = 0
        for kind in [0] * plain + [1] * masked:
            left = left_buf[slot]
            if kind:
                keep = [keep_ref[pl.ds(leaves[2 * slot + half], 1), :].astype(BF) for half in range(2)]
                left = left * jnp.concatenate(keep, axis=1)
            value = jnp.dot(left, right_buf[slot], preferred_element_type=F32)
            rows = pl.ds(at, ROWS)
            if slot:
                out_ref[rows, :] += value
            elif added:
                out_ref[rows, :] = refs[0][rows, :] + value
            else:
                out_ref[rows, :] = value
            at += ROWS


def products(front, me, keep, parts, start=None, plain=True, masked=True):
    blocks = [part[0] for part in parts]
    units = [(i, row, part[1], part[2], part[3] + row) for i, part in enumerate(parts) for row in range(2)]
    out = jax.ShapeDtypeStruct(((plain + masked) * ROWS, SAMPLES), F32)
    anywhere = pl.BlockSpec(memory_space=pl.ANY)
    whole = lambda array: pl.BlockSpec(array.shape, lambda i, s: (0, 0))
    return pl.pallas_call(
        functools.partial(product_kernel, units, plain, masked, start is not None),
        grid_spec=pltpu.PrefetchScalarGridSpec(
            num_scalar_prefetch=1,
            grid=(1,),
            in_specs=[anywhere, whole(keep)] + [anywhere] * len(blocks) + ([] if start is None else [whole(start)]),
            out_specs=whole(out),
            scratch_shapes=[
                pltpu.VMEM((len(units) // 2, ROWS, 2 * WINDOW), BF),
                pltpu.VMEM((len(units) // 2, 2 * WINDOW, SAMPLES), BF),
                pltpu.SemaphoreType.DMA((len(units), 2)),
            ],
        ),
        out_shape=out,
        input_output_aliases={} if start is None else {3 + len(blocks): 0},
        compiler_params=pltpu.CompilerParams(vmem_limit_bytes=VMEM),
        cost_estimate=pl.CostEstimate(
            flops=2 * len(units) * out.shape[0] * WINDOW * SAMPLES,
            bytes_accessed=2 * len(units) * ROWS * WINDOW,
            transcendentals=0,
        ),
    )(me[None], front, keep, *blocks, *([] if start is None else [start]))


def pair_kernel(me_ref, front, mine_ref, yours_ref, names_ref, out_ref, left_buf, right_buf, sems):
    leaves = (me_ref[0], jnp.bitwise_xor(me_ref[0], 1))
    copies = [
        pltpu.make_async_copy(
            front.at[:, pl.ds(pl.multiple_of(window_tile(leaf) * LANES, LANES), WINDOW)],
            left_buf.at[:, pl.ds(half * WINDOW, WINDOW)],
            sems.at[half],
        )
        for half, leaf in enumerate(leaves)
    ]
    for copy in copies:
        copy.start()
    named = jnp.where(lax.broadcasted_iota(jnp.int32, (ROWS, RANK), 0) == names_ref[...], 1.0, 0.0).astype(BF)
    count = jnp.dot(named, jnp.ones((RANK, SAMPLES), BF), preferred_element_type=F32).astype(BF)
    right_buf[...] = jnp.zeros_like(right_buf)
    for half, leaf in enumerate(leaves):
        at = pl.ds(pl.multiple_of(half * WINDOW + window_place(leaf), 32), ROWS)
        right_buf[at, :] = yours_ref[...] * count if half else mine_ref[...]
    for copy in copies:
        copy.wait()
    out_ref[...] = jnp.dot(left_buf[...], right_buf[...], preferred_element_type=F32)


def pair_terms(front, me, mine, yours, names):
    whole = lambda array: pl.BlockSpec(array.shape, lambda i, s: (0, 0))
    return pl.pallas_call(
        pair_kernel,
        grid_spec=pltpu.PrefetchScalarGridSpec(
            num_scalar_prefetch=1,
            grid=(1,),
            in_specs=[pl.BlockSpec(memory_space=pl.ANY), whole(mine), whole(yours), whole(names)],
            out_specs=pl.BlockSpec((ROWS, SAMPLES), lambda i, s: (0, 0)),
            scratch_shapes=[
                pltpu.VMEM((ROWS, 2 * WINDOW), BF),
                pltpu.VMEM((2 * WINDOW, SAMPLES), BF),
                pltpu.SemaphoreType.DMA((2,)),
            ],
        ),
        out_shape=jax.ShapeDtypeStruct((ROWS, SAMPLES), F32),
        compiler_params=pltpu.CompilerParams(vmem_limit_bytes=VMEM),
        cost_estimate=pl.CostEstimate(flops=4 * ROWS * WINDOW * SAMPLES, bytes_accessed=4 * ROWS * WINDOW, transcendentals=0),
    )(me[None], front, mine, yours, names)


def body(front_rows, samples, child_rows, child_owner, child_local, leaf_skeleton, merge_select):
    leaf_total = lax.axis_size("hss")
    myself = lax.axis_index("hss")
    side = jnp.bitwise_and(myself, 1)
    front = front_rows[0]
    skeletons = leaf_skeleton[0]

    own = samples[0]
    turned = [own] + [shifted(own, first(turn)) for turn in (1, 2, 3)]
    lines = [jnp.stack(turned[:2]), jnp.stack(turned[2:])]

    root_slot, keep = fates(myself, merge_select[0], skeletons)

    groups = CHILD // LANES
    owners = lax.reshape(child_owner, (leaf_total * groups, LANES))
    targets = lax.reshape(child_local, (leaf_total * groups, LANES))
    my_owners = lax.dynamic_slice_in_dim(owners, myself * groups, groups, 0).reshape(-1)
    my_targets = my_owners * ROWS + lax.dynamic_slice_in_dim(targets, myself * groups, groups, 0).reshape(-1)
    earlier = iota(CHILD)[:, None] < iota(CHILD)[None, :]
    my_slots = jnp.sum(((my_owners[:, None] == my_owners[None, :]) & earlier).astype(jnp.int32), axis=0)
    destination = my_owners * CAP + my_slots
    send_select = (iota(leaf_total * CAP)[:, None] == destination[None, :]).astype(BF)
    outgoing = jnp.dot(send_select, child_rows[0], preferred_element_type=F32).astype(BF)
    all_rows = iota(leaf_total)[:, None] * ROWS + skeletons + 1
    root_ids = jnp.sum(
        jnp.where(root_slot[:, :, None] == iota(RANK)[None, None, :] + 1, all_rows[:, :, None], 0), axis=(0, 1)
    ) - 1
    root_hits = (root_ids[:, None] == my_targets[None, :]).astype(BF)
    root_arrivals = jnp.dot(root_hits, child_rows[0], preferred_element_type=F32)

    lines, outgoing = lax.optimization_barrier((lines, outgoing))
    far_a = shifted(lines[0], second(2))
    near_b = shifted(lines[1], second(1))
    near_a = shifted(lines[0], second(1))
    far_b = shifted(lines[1], second(2))

    def both(block, step, turn):
        return [(block, 0, step, turn), (shifted(block, cores), 1, step, turn)]

    parts = both(lines[0], 0, 0) + both(lines[1], 0, 2)
    total = products(front, myself, keep, parts)
    yours = parts[1][0][0]
    far_a, near_b, outgoing, total = lax.optimization_barrier((far_a, near_b, outgoing, total))
    incoming = lax.all_to_all(
        outgoing.reshape(leaf_total, CAP, SAMPLES), "hss", split_axis=0, concat_axis=0, tiled=True
    ).reshape(leaf_total * CAP, SAMPLES)
    opposite = [shifted(far_a, second(1)), shifted(near_b, second(2))]
    parts = both(far_a, 2, 0) + both(near_b, 1, 2) + both(near_a, 1, 0) + both(far_b, 2, 2)
    total = products(front, myself, keep, parts, total)
    opposite, total = lax.optimization_barrier((opposite, total))
    full, root = total[:ROWS], total[ROWS:]
    parts = both(opposite[0], 3, 0) + both(opposite[1], 3, 2)
    root = products(front, myself, keep, parts, root, plain=False)
    my_root_slot = pick_index(root_slot, myself)
    my_skeleton = pick_index(skeletons, myself)
    root_rows = jnp.sum(jnp.where(my_root_slot[:, None] == iota(RANK)[None, :] + 1, my_skeleton[:, None] + 1, 0), axis=0) - 1
    root_pick = (root_rows[:, None] == iota(ROWS)[None, :]).astype(F32)
    root = jnp.dot(root_pick, root, precision=lax.Precision.HIGHEST) + root_arrivals

    half = RANK // 2
    kept = jnp.where(side == 0, root[:half], root[half:])
    kept = kept + shifted(jnp.where(side == 0, root[half:], root[:half]), cores)
    kept, full = lax.optimization_barrier((kept, full))
    full = products(front, myself, keep, parts[:2], full, masked=False)
    kept = total_over_ring(kept, along_z)
    kept, full = lax.optimization_barrier((kept, full))
    full = products(front, myself, keep, parts[2:], full, masked=False)
    kept = total_over_ring(kept, along_x)
    other = shifted(kept, cores)
    root = jnp.concatenate([jnp.where(side == 0, kept, other), jnp.where(side == 0, other, kept)], axis=0)

    hits = (owners == myself).astype(BF)
    before = (iota(LANES)[:, None] < iota(LANES)[None, :]).astype(BF)
    row = iota(leaf_total * groups)
    above = ((row[:, None] // groups == row[None, :] // groups) & (row[:, None] > row[None, :])).astype(BF)
    counts = jnp.dot(hits, jnp.ones((LANES, LANES), BF), preferred_element_type=F32).astype(BF)
    order = jnp.dot(hits, before, preferred_element_type=F32) + jnp.dot(above, counts, preferred_element_type=F32)
    placed = jnp.where(owners == myself, order.astype(jnp.int32), CAP).reshape(leaf_total, groups, LANES)
    slot_hits = placed[:, :, :, None] == iota(CAP)
    slot_rows = jnp.sum(jnp.where(slot_hits, targets.reshape(leaf_total, groups, LANES)[:, :, :, None] + 1, 0), axis=(1, 2)) - 1
    selector = (iota(ROWS)[:, None] == slot_rows.reshape(-1)[None, :]).astype(BF)
    full = full + jnp.dot(selector, incoming, preferred_element_type=F32)
    parent = full.astype(BF)

    pair_choice = pick_index(merge_select[0], jnp.right_shift(myself, 1)) - side * RANK
    pair_rows = jnp.sum(jnp.where(iota(RANK)[:, None] == pair_choice[None, :], my_skeleton[:, None] + 1, 0), axis=0) - 1
    pair_pick = (pair_rows[:, None] == iota(ROWS)[None, :]).astype(F32)
    pair_gone = pair_terms(front, myself, own, yours, pick_index(skeletons, cores(myself))[None])
    pair = jnp.dot(pair_pick, full - pair_gone, precision=lax.Precision.HIGHEST)
    pair = pair + shifted(pair, cores)
    return (parent[None], pair[None], root[None])


def solution(mesh):
    in_specs = (
        P("front", "hss", None),
        P("front", "hss", None),
        P("front", "hss", None),
        P("front", None, None),
        P("front", None),
        P("front", None, None),
        P("front", None, None),
    )
    out_specs = (P("front", "hss", None), P("front", "hss", None), P("front", None, None))
    return jax.shard_map(body, mesh=mesh, in_specs=in_specs, out_specs=out_specs, check_vma=False)
```

```python
import functools

import jax
import jax.numpy as jnp
from jax import lax
from jax.experimental import pallas as pl
from jax.experimental.pallas import tpu as pltpu
from jax.sharding import PartitionSpec as P

ROWS = 608
SAMPLES = 256
RANK = 128
CHILD = 512
CAP = 64
BF = jnp.bfloat16
F32 = jnp.float32
LANES = 128
SUBLANES = 16
WINDOW = 768
PLACES = (0, 96, 64, 160)
RING = 4
TURNS = (0, 1, 3, 2)
AHEAD = 2
VMEM = 42 << 20


def pick_index(table, position):
    return lax.dynamic_index_in_dim(table, position, 0, keepdims=False)


def iota(n):
    return jnp.arange(n, dtype=jnp.int32)


def shifted(x, move):
    return lax.ppermute(x, "hss", [(i, move(i)) for i in range(lax.axis_size("hss"))])


def cores(i):
    return i ^ 1


def along_z(turn):
    return lambda i: i ^ 2 * TURNS[turn]


def along_x(turn):
    return lambda i: i ^ 8 * TURNS[turn]


def first(turn):
    return lambda i: along_x(turn)(i) if i % 2 else along_z(turn)(i)


def second(turn):
    return lambda i: along_z(turn)(i) if i % 2 else along_x(turn)(i)


def total_over_ring(x, along):
    near, far, opposite = [shifted(x, along(turn)) for turn in (1, 2, 3)]
    return (x + near) + (far + opposite)


def fate_kernel(me_ref, select_ref, skeleton_ref, slots_ref, keep_ref):
    me = me_ref[0]
    row = lax.broadcasted_iota(jnp.int32, (SUBLANES, RANK), 0)
    once = jnp.where(row == 0, 1.0, 0.0)
    carried = [jnp.where(row == 1, lax.broadcasted_iota(jnp.int32, (SUBLANES, RANK), 1) + 1, 0).astype(F32)]
    place = lax.broadcasted_iota(jnp.int32, (2 * RANK, RANK), 0)
    at = select_ref.shape[0]
    while at > 0:
        at -= len(carried)
        below = []
        for node, values in enumerate(carried):
            hit = jnp.where(place == select_ref[at + node : at + node + 1, :], 1.0, 0.0).astype(BF)
            spread = lax.dot_general((values + once).astype(BF), hit, (((1,), (1,)), ((), ())), preferred_element_type=F32)
            below += [spread[:, :RANK], spread[:, RANK:]]
        carried = below
    gone = []
    for leaf, values in enumerate(carried):
        slots_ref[leaf : leaf + 1, :] = values[1:2, :].astype(jnp.int32)
        apart = jnp.bitwise_xor(me, leaf)
        level = sum([jnp.where(apart >= (2 << h), 1, 0) for h in range(4)])
        names = skeleton_ref[leaf : leaf + 1, :]
        gone.append(jnp.where(values[0:1, :].astype(jnp.int32) >= level, names, -WINDOW))
    gone = jnp.concatenate(gone + [gone[0]] * (RANK - len(gone)), axis=0).T
    lane = lax.broadcasted_iota(jnp.int32, (RANK, WINDOW), 1)
    for leaf in range(len(carried)):
        named = jnp.where(lane - PLACES[leaf % 4] == gone[:, leaf : leaf + 1], 1.0, 0.0)
        keep = 1.0 - jnp.max(named, axis=0, keepdims=True)
        keep_ref[leaf : leaf + 1, :] = keep * jnp.where(me == leaf, 0.0, 1.0)


def fates(me, selections, skeletons):
    leaves = skeletons.shape[0]
    return pl.pallas_call(
        fate_kernel,
        in_specs=[pl.BlockSpec(memory_space=pltpu.SMEM), pl.BlockSpec(), pl.BlockSpec()],
        out_shape=[jax.ShapeDtypeStruct((leaves, RANK), jnp.int32), jax.ShapeDtypeStruct((leaves, WINDOW), F32)],
        compiler_params=pltpu.CompilerParams(vmem_limit_bytes=VMEM),
        cost_estimate=pl.CostEstimate(flops=leaves << 20, bytes_accessed=leaves << 12, transcendentals=0),
    )(me[None], selections, skeletons)


def window_tile(leaf):
    return 19 * leaf // 4 - jnp.where(leaf % 4 == 3, 1, 0)


def window_place(leaf):
    kind = leaf % 4
    return jnp.where(kind == 0, PLACES[0], jnp.where(kind == 1, PLACES[1], jnp.where(kind == 2, PLACES[2], PLACES[3])))


def leaf_of(me, whose, step, j):
    by_first = 2 * TURNS[j] + 8 * TURNS[step]
    by_second = 8 * TURNS[j] + 2 * TURNS[step]
    side = jnp.bitwise_and(me, 1)
    moved = jnp.where(side == whose, by_first, by_second)
    return jnp.bitwise_xor(jnp.bitwise_xor(me, whose), moved)


def product_kernel(units, plain, masked, added, me_ref, front, keep_ref, *refs):
    blocks, refs = refs[: units[-1][0] + 1], refs[units[-1][0] + 1 :]
    out_ref, left_buf, right_buf, sems = refs[-4:]
    leaves = [leaf_of(me_ref[0], *unit[2:]) for unit in units]

    def copies(u):
        block, row = units[u][:2]
        slot, half = u // 2 % (AHEAD + 1), u % 2
        columns = pl.ds(pl.multiple_of(window_tile(leaves[u]) * LANES, LANES), WINDOW)
        rows = pl.ds(pl.multiple_of(half * WINDOW + window_place(leaves[u]), 32), ROWS)
        return (
            pltpu.make_async_copy(
                front.at[:, columns], left_buf.at[slot, :, pl.ds(half * WINDOW, WINDOW)], sems.at[u, 0]
            ),
            pltpu.make_async_copy(blocks[block].at[row], right_buf.at[slot, rows, :], sems.at[u, 1]),
        )

    def begin(slot):
        for u in (2 * slot, 2 * slot + 1):
            edge, into = (u % 2) * WINDOW, slot % (AHEAD + 1)
            right_buf[into, edge : edge + PLACES[-1], :] = jnp.zeros((PLACES[-1], SAMPLES), BF)
            right_buf[into, edge + ROWS : edge + WINDOW, :] = jnp.zeros((WINDOW - ROWS, SAMPLES), BF)
            for copy in copies(u):
                copy.start()

    slots = len(units) // 2
    for slot in range(min(AHEAD, slots)):
        begin(slot)
    for slot in range(slots):
        for u in (2 * slot, 2 * slot + 1):
            for copy in copies(u):
                copy.wait()
        if slot + AHEAD < slots:
            begin(slot + AHEAD)
        at = 0
        for kind in [0] * plain + [1] * masked:
            left = left_buf[slot % (AHEAD + 1)]
            if kind:
                keep = [keep_ref[pl.ds(leaves[2 * slot + half], 1), :].astype(BF) for half in range(2)]
                left = left * jnp.concatenate(keep, axis=1)
            value = jnp.dot(left, right_buf[slot % (AHEAD + 1)], preferred_element_type=F32)
            rows = pl.ds(at, ROWS)
            if slot:
                out_ref[rows, :] += value
            elif added:
                out_ref[rows, :] = refs[0][rows, :] + value
            else:
                out_ref[rows, :] = value
            at += ROWS


def products(front, me, keep, parts, start=None, plain=True, masked=True):
    blocks = [part[0] for part in parts]
    units = [(i, row, part[1], part[2], part[3] + row) for i, part in enumerate(parts) for row in range(2)]
    out = jax.ShapeDtypeStruct(((plain + masked) * ROWS, SAMPLES), F32)
    anywhere = pl.BlockSpec(memory_space=pl.ANY)
    whole = lambda array: pl.BlockSpec(array.shape, lambda i, s: (0, 0))
    return pl.pallas_call(
        functools.partial(product_kernel, units, plain, masked, start is not None),
        grid_spec=pltpu.PrefetchScalarGridSpec(
            num_scalar_prefetch=1,
            grid=(1,),
            in_specs=[anywhere, whole(keep)] + [anywhere] * len(blocks) + ([] if start is None else [whole(start)]),
            out_specs=whole(out),
            scratch_shapes=[
                pltpu.VMEM((AHEAD + 1, ROWS, 2 * WINDOW), BF),
                pltpu.VMEM((AHEAD + 1, 2 * WINDOW, SAMPLES), BF),
                pltpu.SemaphoreType.DMA((len(units), 2)),
            ],
        ),
        out_shape=out,
        input_output_aliases={} if start is None else {3 + len(blocks): 0},
        compiler_params=pltpu.CompilerParams(vmem_limit_bytes=VMEM),
        cost_estimate=pl.CostEstimate(
            flops=2 * len(units) * out.shape[0] * WINDOW * SAMPLES,
            bytes_accessed=2 * len(units) * ROWS * WINDOW,
            transcendentals=0,
        ),
    )(me[None], front, keep, *blocks, *([] if start is None else [start]))


def pair_kernel(me_ref, front, mine_ref, yours_ref, names_ref, out_ref, left_buf, right_buf, sems):
    leaves = (me_ref[0], jnp.bitwise_xor(me_ref[0], 1))
    copies = [
        pltpu.make_async_copy(
            front.at[:, pl.ds(pl.multiple_of(window_tile(leaf) * LANES, LANES), WINDOW)],
            left_buf.at[:, pl.ds(half * WINDOW, WINDOW)],
            sems.at[half],
        )
        for half, leaf in enumerate(leaves)
    ]
    for copy in copies:
        copy.start()
    named = jnp.where(lax.broadcasted_iota(jnp.int32, (ROWS, RANK), 0) == names_ref[...], 1.0, 0.0).astype(BF)
    count = jnp.dot(named, jnp.ones((RANK, SAMPLES), BF), preferred_element_type=F32).astype(BF)
    right_buf[...] = jnp.zeros_like(right_buf)
    for half, leaf in enumerate(leaves):
        at = pl.ds(pl.multiple_of(half * WINDOW + window_place(leaf), 32), ROWS)
        right_buf[at, :] = yours_ref[...] * count if half else mine_ref[...]
    for copy in copies:
        copy.wait()
    out_ref[...] = jnp.dot(left_buf[...], right_buf[...], preferred_element_type=F32)


def pair_terms(front, me, mine, yours, names):
    whole = lambda array: pl.BlockSpec(array.shape, lambda i, s: (0, 0))
    return pl.pallas_call(
        pair_kernel,
        grid_spec=pltpu.PrefetchScalarGridSpec(
            num_scalar_prefetch=1,
            grid=(1,),
            in_specs=[pl.BlockSpec(memory_space=pl.ANY), whole(mine), whole(yours), whole(names)],
            out_specs=pl.BlockSpec((ROWS, SAMPLES), lambda i, s: (0, 0)),
            scratch_shapes=[
                pltpu.VMEM((ROWS, 2 * WINDOW), BF),
                pltpu.VMEM((2 * WINDOW, SAMPLES), BF),
                pltpu.SemaphoreType.DMA((2,)),
            ],
        ),
        out_shape=jax.ShapeDtypeStruct((ROWS, SAMPLES), F32),
        compiler_params=pltpu.CompilerParams(vmem_limit_bytes=VMEM),
        cost_estimate=pl.CostEstimate(flops=4 * ROWS * WINDOW * SAMPLES, bytes_accessed=4 * ROWS * WINDOW, transcendentals=0),
    )(me[None], front, mine, yours, names)


def body(front_rows, samples, child_rows, child_owner, child_local, leaf_skeleton, merge_select):
    leaf_total = lax.axis_size("hss")
    myself = lax.axis_index("hss")
    side = jnp.bitwise_and(myself, 1)
    front = front_rows[0]
    skeletons = leaf_skeleton[0]

    own = samples[0]
    turned = [own] + [shifted(own, first(turn)) for turn in (1, 2, 3)]
    root_slot, keep = fates(myself, merge_select[0], skeletons)

    groups = CHILD // LANES
    owners = lax.reshape(child_owner, (leaf_total * groups, LANES))
    targets = lax.reshape(child_local, (leaf_total * groups, LANES))
    my_owners = lax.dynamic_slice_in_dim(owners, myself * groups, groups, 0).reshape(-1)
    my_targets = my_owners * ROWS + lax.dynamic_slice_in_dim(targets, myself * groups, groups, 0).reshape(-1)
    earlier = iota(CHILD)[:, None] < iota(CHILD)[None, :]
    my_slots = jnp.sum(((my_owners[:, None] == my_owners[None, :]) & earlier).astype(jnp.int32), axis=0)
    destination = my_owners * CAP + my_slots
    send_select = (iota(leaf_total * CAP)[:, None] == destination[None, :]).astype(BF)
    outgoing = jnp.dot(send_select, child_rows[0], preferred_element_type=F32).astype(BF)
    all_rows = iota(leaf_total)[:, None] * ROWS + skeletons + 1
    root_ids = jnp.sum(
        jnp.where(root_slot[:, :, None] == iota(RANK)[None, None, :] + 1, all_rows[:, :, None], 0), axis=(0, 1)
    ) - 1
    root_hits = (root_ids[:, None] == my_targets[None, :]).astype(BF)
    root_arrivals = jnp.dot(root_hits, child_rows[0], preferred_element_type=F32)

    turned, keep, outgoing, root_arrivals = lax.optimization_barrier((turned, keep, outgoing, root_arrivals))
    lines = [jnp.stack(turned[:2]), jnp.stack(turned[2:])]
    far_a = shifted(lines[0], second(2))
    near_b = shifted(lines[1], second(1))

    def both(block, step, turn):
        return [(block, 0, step, turn), (shifted(block, cores), 1, step, turn)]

    parts = both(lines[0], 0, 0) + both(lines[1], 0, 2)
    total = products(front, myself, keep, parts)
    yours = parts[1][0][0]
    far_a, near_b, lines, total = lax.optimization_barrier((far_a, near_b, lines, total))
    opposite = [shifted(far_a, second(1)), shifted(near_b, second(2))]
    near_a = shifted(lines[0], second(1))
    far_b = shifted(lines[1], second(2))
    total = products(front, myself, keep, both(far_a, 2, 0) + both(near_b, 1, 2), total)
    outgoing, near_a, far_b, total = lax.optimization_barrier((outgoing, near_a, far_b, total))
    incoming = lax.all_to_all(
        outgoing.reshape(leaf_total, CAP, SAMPLES), "hss", split_axis=0, concat_axis=0, tiled=True
    ).reshape(leaf_total * CAP, SAMPLES)
    total = products(front, myself, keep, both(near_a, 1, 0) + both(far_b, 2, 2), total)
    opposite, total = lax.optimization_barrier((opposite, total))
    total = products(front, myself, keep, both(opposite[0], 3, 0) + both(opposite[1], 3, 2), total)
    total, incoming = lax.optimization_barrier((total, incoming))
    full, root = total[:ROWS], total[ROWS:]
    my_root_slot = pick_index(root_slot, myself)
    my_skeleton = pick_index(skeletons, myself)
    root_rows = jnp.sum(jnp.where(my_root_slot[:, None] == iota(RANK)[None, :] + 1, my_skeleton[:, None] + 1, 0), axis=0) - 1
    root_pick = (root_rows[:, None] == iota(ROWS)[None, :]).astype(F32)
    root = jnp.dot(root_pick, root, precision=lax.Precision.HIGHEST) + root_arrivals

    half = RANK // 2
    kept = jnp.where(side == 0, root[:half], root[half:])
    kept = kept + shifted(jnp.where(side == 0, root[half:], root[:half]), cores)
    kept, owners, targets, incoming = lax.optimization_barrier((kept, owners, targets, incoming))
    kept = total_over_ring(kept, along_z)
    kept, yours = lax.optimization_barrier((kept, yours))
    kept = total_over_ring(kept, along_x)
    other = shifted(kept, cores)
    root = jnp.concatenate([jnp.where(side == 0, kept, other), jnp.where(side == 0, other, kept)], axis=0)

    hits = (owners == myself).astype(BF)
    before = (iota(LANES)[:, None] < iota(LANES)[None, :]).astype(BF)
    row = iota(leaf_total * groups)
    above = ((row[:, None] // groups == row[None, :] // groups) & (row[:, None] > row[None, :])).astype(BF)
    counts = jnp.dot(hits, jnp.ones((LANES, LANES), BF), preferred_element_type=F32).astype(BF)
    order = jnp.dot(hits, before, preferred_element_type=F32) + jnp.dot(above, counts, preferred_element_type=F32)
    placed = jnp.where(owners == myself, order.astype(jnp.int32), CAP).reshape(leaf_total, groups, LANES)
    slot_hits = placed[:, :, :, None] == iota(CAP)
    slot_rows = jnp.sum(jnp.where(slot_hits, targets.reshape(leaf_total, groups, LANES)[:, :, :, None] + 1, 0), axis=(1, 2)) - 1
    selector = (iota(ROWS)[:, None] == slot_rows.reshape(-1)[None, :]).astype(BF)
    full = full + jnp.dot(selector, incoming, preferred_element_type=F32)
    parent = full.astype(BF)

    pair_choice = pick_index(merge_select[0], jnp.right_shift(myself, 1)) - side * RANK
    pair_rows = jnp.sum(jnp.where(iota(RANK)[:, None] == pair_choice[None, :], my_skeleton[:, None] + 1, 0), axis=0) - 1
    pair_pick = (pair_rows[:, None] == iota(ROWS)[None, :]).astype(F32)
    pair_gone = pair_terms(front, myself, own, yours, pick_index(skeletons, cores(myself))[None])
    pair = jnp.dot(pair_pick, full - pair_gone, precision=lax.Precision.HIGHEST)
    pair = pair + shifted(pair, cores)
    return (parent[None], pair[None], root[None])


def solution(mesh):
    in_specs = (
        P("front", "hss", None),
        P("front", "hss", None),
        P("front", "hss", None),
        P("front", None, None),
        P("front", None),
        P("front", None, None),
        P("front", None, None),
    )
    out_specs = (P("front", "hss", None), P("front", "hss", None), P("front", None, None))
    return jax.shard_map(body, mesh=mesh, in_specs=in_specs, out_specs=out_specs, check_vma=False)
```

```python
import functools

import jax
import jax.numpy as jnp
from jax import lax
from jax.experimental import pallas as pl
from jax.experimental.pallas import tpu as pltpu
from jax.sharding import PartitionSpec as P

ROWS = 608
SAMPLES = 256
RANK = 128
CHILD = 512
CAP = 64
BF = jnp.bfloat16
F32 = jnp.float32
LANES = 128
SUBLANES = 16
WINDOW = 768
PLACES = (0, 96, 64, 160)
RING = 4
TURNS = (0, 1, 3, 2)
AHEAD = 2
VMEM = 42 << 20


def pick_index(table, position):
    return lax.dynamic_index_in_dim(table, position, 0, keepdims=False)


def iota(n):
    return jnp.arange(n, dtype=jnp.int32)


def shifted(x, move):
    return lax.ppermute(x, "hss", [(i, move(i)) for i in range(lax.axis_size("hss"))])


def cores(i):
    return i ^ 1


def along_z(turn):
    return lambda i: i ^ 2 * TURNS[turn]


def along_x(turn):
    return lambda i: i ^ 8 * TURNS[turn]


def first(turn):
    return lambda i: along_x(turn)(i) if i % 2 else along_z(turn)(i)


def second(turn):
    return lambda i: along_z(turn)(i) if i % 2 else along_x(turn)(i)


def total_over_ring(x, along):
    near, far, opposite = [shifted(x, along(turn)) for turn in (1, 2, 3)]
    return (x + near) + (far + opposite)


def fate_kernel(me_ref, select_ref, skeleton_ref, slots_ref, keep_ref):
    me = me_ref[0]
    row = lax.broadcasted_iota(jnp.int32, (SUBLANES, RANK), 0)
    once = jnp.where(row == 0, 1.0, 0.0)
    carried = [jnp.where(row == 1, lax.broadcasted_iota(jnp.int32, (SUBLANES, RANK), 1) + 1, 0).astype(F32)]
    place = lax.broadcasted_iota(jnp.int32, (2 * RANK, RANK), 0)
    at = select_ref.shape[0]
    while at > 0:
        at -= len(carried)
        below = []
        for node, values in enumerate(carried):
            hit = jnp.where(place == select_ref[at + node : at + node + 1, :], 1.0, 0.0).astype(BF)
            spread = lax.dot_general((values + once).astype(BF), hit, (((1,), (1,)), ((), ())), preferred_element_type=F32)
            below += [spread[:, :RANK], spread[:, RANK:]]
        carried = below
    gone = []
    for leaf, values in enumerate(carried):
        slots_ref[leaf : leaf + 1, :] = values[1:2, :].astype(jnp.int32)
        apart = jnp.bitwise_xor(me, leaf)
        level = sum([jnp.where(apart >= (2 << h), 1, 0) for h in range(4)])
        names = skeleton_ref[leaf : leaf + 1, :]
        gone.append(jnp.where(values[0:1, :].astype(jnp.int32) >= level, names, -WINDOW))
    gone = jnp.concatenate(gone + [gone[0]] * (RANK - len(gone)), axis=0).T
    lane = lax.broadcasted_iota(jnp.int32, (RANK, WINDOW), 1)
    for leaf in range(len(carried)):
        named = jnp.where(lane - PLACES[leaf % 4] == gone[:, leaf : leaf + 1], 1.0, 0.0)
        keep = 1.0 - jnp.max(named, axis=0, keepdims=True)
        keep_ref[leaf : leaf + 1, :] = keep * jnp.where(me == leaf, 0.0, 1.0)


def fates(me, selections, skeletons):
    leaves = skeletons.shape[0]
    return pl.pallas_call(
        fate_kernel,
        in_specs=[pl.BlockSpec(memory_space=pltpu.SMEM), pl.BlockSpec(), pl.BlockSpec()],
        out_shape=[jax.ShapeDtypeStruct((leaves, RANK), jnp.int32), jax.ShapeDtypeStruct((leaves, WINDOW), F32)],
        compiler_params=pltpu.CompilerParams(vmem_limit_bytes=VMEM),
        cost_estimate=pl.CostEstimate(flops=leaves << 20, bytes_accessed=leaves << 12, transcendentals=0),
    )(me[None], selections, skeletons)


def window_tile(leaf):
    return 19 * leaf // 4 - jnp.where(leaf % 4 == 3, 1, 0)


def window_place(leaf):
    kind = leaf % 4
    return jnp.where(kind == 0, PLACES[0], jnp.where(kind == 1, PLACES[1], jnp.where(kind == 2, PLACES[2], PLACES[3])))


def leaf_of(me, whose, step, j):
    by_first = 2 * TURNS[j] + 8 * TURNS[step]
    by_second = 8 * TURNS[j] + 2 * TURNS[step]
    side = jnp.bitwise_and(me, 1)
    moved = jnp.where(side == whose, by_first, by_second)
    return jnp.bitwise_xor(jnp.bitwise_xor(me, whose), moved)


def product_kernel(units, plain, masked, added, me_ref, front, keep_ref, *refs):
    blocks, refs = refs[: units[-1][0] + 1], refs[units[-1][0] + 1 :]
    out_ref, left_buf, right_buf, sems = refs[-4:]
    leaves = [leaf_of(me_ref[0], *unit[2:]) for unit in units]

    def copies(u):
        block, row = units[u][:2]
        slot, half = u // 2 % (AHEAD + 1), u % 2
        columns = pl.ds(pl.multiple_of(window_tile(leaves[u]) * LANES, LANES), WINDOW)
        rows = pl.ds(pl.multiple_of(half * WINDOW + window_place(leaves[u]), 32), ROWS)
        return (
            pltpu.make_async_copy(
                front.at[:, columns], left_buf.at[slot, :, pl.ds(half * WINDOW, WINDOW)], sems.at[u, 0]
            ),
            pltpu.make_async_copy(blocks[block].at[row], right_buf.at[slot, rows, :], sems.at[u, 1]),
        )

    def begin(slot):
        for u in (2 * slot, 2 * slot + 1):
            edge, into = (u % 2) * WINDOW, slot % (AHEAD + 1)
            right_buf[into, edge : edge + PLACES[-1], :] = jnp.zeros((PLACES[-1], SAMPLES), BF)
            right_buf[into, edge + ROWS : edge + WINDOW, :] = jnp.zeros((WINDOW - ROWS, SAMPLES), BF)
            for copy in copies(u):
                copy.start()

    slots = len(units) // 2
    for slot in range(min(AHEAD, slots)):
        begin(slot)
    for slot in range(slots):
        for u in (2 * slot, 2 * slot + 1):
            for copy in copies(u):
                copy.wait()
        if slot + AHEAD < slots:
            begin(slot + AHEAD)
        at = 0
        for kind in [0] * plain + [1] * masked:
            left = left_buf[slot % (AHEAD + 1)]
            if kind:
                keep = [keep_ref[pl.ds(leaves[2 * slot + half], 1), :].astype(BF) for half in range(2)]
                left = left * jnp.concatenate(keep, axis=1)
            value = jnp.dot(left, right_buf[slot % (AHEAD + 1)], preferred_element_type=F32)
            rows = pl.ds(at, ROWS)
            if slot:
                out_ref[rows, :] += value
            elif added:
                out_ref[rows, :] = refs[0][rows, :] + value
            else:
                out_ref[rows, :] = value
            at += ROWS


def products(front, me, keep, parts, start=None, plain=True, masked=True):
    blocks = [part[0] for part in parts]
    units = [(i, row, part[1], part[2], part[3] + row) for i, part in enumerate(parts) for row in range(2)]
    out = jax.ShapeDtypeStruct(((plain + masked) * ROWS, SAMPLES), F32)
    anywhere = pl.BlockSpec(memory_space=pl.ANY)
    whole = lambda array: pl.BlockSpec(array.shape, lambda i, s: (0, 0))
    return pl.pallas_call(
        functools.partial(product_kernel, units, plain, masked, start is not None),
        grid_spec=pltpu.PrefetchScalarGridSpec(
            num_scalar_prefetch=1,
            grid=(1,),
            in_specs=[anywhere, whole(keep)] + [anywhere] * len(blocks) + ([] if start is None else [whole(start)]),
            out_specs=whole(out),
            scratch_shapes=[
                pltpu.VMEM((AHEAD + 1, ROWS, 2 * WINDOW), BF),
                pltpu.VMEM((AHEAD + 1, 2 * WINDOW, SAMPLES), BF),
                pltpu.SemaphoreType.DMA((len(units), 2)),
            ],
        ),
        out_shape=out,
        input_output_aliases={} if start is None else {3 + len(blocks): 0},
        compiler_params=pltpu.CompilerParams(vmem_limit_bytes=VMEM),
        cost_estimate=pl.CostEstimate(
            flops=len(units) * out.shape[0] * WINDOW * SAMPLES // 2,
            bytes_accessed=len(units) * ROWS * WINDOW // 2,
            transcendentals=0,
        ),
    )(me[None], front, keep, *blocks, *([] if start is None else [start]))


def pair_kernel(me_ref, front, mine_ref, yours_ref, names_ref, out_ref, left_buf, right_buf, sems):
    leaves = (me_ref[0], jnp.bitwise_xor(me_ref[0], 1))
    copies = [
        pltpu.make_async_copy(
            front.at[:, pl.ds(pl.multiple_of(window_tile(leaf) * LANES, LANES), WINDOW)],
            left_buf.at[:, pl.ds(half * WINDOW, WINDOW)],
            sems.at[half],
        )
        for half, leaf in enumerate(leaves)
    ]
    for copy in copies:
        copy.start()
    named = jnp.where(lax.broadcasted_iota(jnp.int32, (ROWS, RANK), 0) == names_ref[...], 1.0, 0.0).astype(BF)
    count = jnp.dot(named, jnp.ones((RANK, SAMPLES), BF), preferred_element_type=F32).astype(BF)
    right_buf[...] = jnp.zeros_like(right_buf)
    for half, leaf in enumerate(leaves):
        at = pl.ds(pl.multiple_of(half * WINDOW + window_place(leaf), 32), ROWS)
        right_buf[at, :] = yours_ref[...] * count if half else mine_ref[...]
    for copy in copies:
        copy.wait()
    out_ref[...] = jnp.dot(left_buf[...], right_buf[...], preferred_element_type=F32)


def pair_terms(front, me, mine, yours, names):
    whole = lambda array: pl.BlockSpec(array.shape, lambda i, s: (0, 0))
    return pl.pallas_call(
        pair_kernel,
        grid_spec=pltpu.PrefetchScalarGridSpec(
            num_scalar_prefetch=1,
            grid=(1,),
            in_specs=[pl.BlockSpec(memory_space=pl.ANY), whole(mine), whole(yours), whole(names)],
            out_specs=pl.BlockSpec((ROWS, SAMPLES), lambda i, s: (0, 0)),
            scratch_shapes=[
                pltpu.VMEM((ROWS, 2 * WINDOW), BF),
                pltpu.VMEM((2 * WINDOW, SAMPLES), BF),
                pltpu.SemaphoreType.DMA((2,)),
            ],
        ),
        out_shape=jax.ShapeDtypeStruct((ROWS, SAMPLES), F32),
        compiler_params=pltpu.CompilerParams(vmem_limit_bytes=VMEM),
        cost_estimate=pl.CostEstimate(flops=4 * ROWS * WINDOW * SAMPLES, bytes_accessed=4 * ROWS * WINDOW, transcendentals=0),
    )(me[None], front, mine, yours, names)


def body(front_rows, samples, child_rows, child_owner, child_local, leaf_skeleton, merge_select):
    leaf_total = lax.axis_size("hss")
    myself = lax.axis_index("hss")
    side = jnp.bitwise_and(myself, 1)
    front = front_rows[0]
    skeletons = leaf_skeleton[0]

    own = samples[0]
    turned = [own] + [shifted(own, first(turn)) for turn in (1, 2, 3)]
    root_slot, keep = fates(myself, merge_select[0], skeletons)

    groups = CHILD // LANES
    owners = lax.reshape(child_owner, (leaf_total * groups, LANES))
    targets = lax.reshape(child_local, (leaf_total * groups, LANES))
    my_owners = lax.dynamic_slice_in_dim(owners, myself * groups, groups, 0).reshape(-1)
    my_targets = my_owners * ROWS + lax.dynamic_slice_in_dim(targets, myself * groups, groups, 0).reshape(-1)
    earlier = iota(CHILD)[:, None] < iota(CHILD)[None, :]
    my_slots = jnp.sum(((my_owners[:, None] == my_owners[None, :]) & earlier).astype(jnp.int32), axis=0)
    destination = my_owners * CAP + my_slots
    send_select = (iota(leaf_total * CAP)[:, None] == destination[None, :]).astype(BF)
    outgoing = jnp.dot(send_select, child_rows[0], preferred_element_type=F32).astype(BF)
    all_rows = iota(leaf_total)[:, None] * ROWS + skeletons + 1
    root_ids = jnp.sum(
        jnp.where(root_slot[:, :, None] == iota(RANK)[None, None, :] + 1, all_rows[:, :, None], 0), axis=(0, 1)
    ) - 1
    root_hits = (root_ids[:, None] == my_targets[None, :]).astype(BF)
    root_arrivals = jnp.dot(root_hits, child_rows[0], preferred_element_type=F32)

    turned, keep, outgoing, root_arrivals = lax.optimization_barrier((turned, keep, outgoing, root_arrivals))
    lines = [jnp.stack(turned[:2]), jnp.stack(turned[2:])]
    far_a = shifted(lines[0], second(2))
    near_b = shifted(lines[1], second(1))

    def both(block, step, turn):
        return [(block, 0, step, turn), (shifted(block, cores), 1, step, turn)]

    parts = both(lines[0], 0, 0) + both(lines[1], 0, 2)
    total = products(front, myself, keep, parts)
    yours = parts[1][0][0]
    far_a, near_b, lines, total = lax.optimization_barrier((far_a, near_b, lines, total))
    opposite = [shifted(far_a, second(1)), shifted(near_b, second(2))]
    near_a = shifted(lines[0], second(1))
    far_b = shifted(lines[1], second(2))
    total = products(front, myself, keep, both(far_a, 2, 0) + both(near_b, 1, 2), total)
    outgoing, total = lax.optimization_barrier((outgoing, total))
    near_a, far_b, opposite, total = lax.optimization_barrier((near_a, far_b, opposite, total))
    incoming = lax.all_to_all(
        outgoing.reshape(leaf_total, CAP, SAMPLES), "hss", split_axis=0, concat_axis=0, tiled=True
    ).reshape(leaf_total * CAP, SAMPLES)
    total = products(front, myself, keep, both(near_a, 1, 0) + both(far_b, 2, 2), total)
    total = products(front, myself, keep, both(opposite[0], 3, 0) + both(opposite[1], 3, 2), total)
    total, incoming = lax.optimization_barrier((total, incoming))
    full, root = total[:ROWS], total[ROWS:]
    my_root_slot = pick_index(root_slot, myself)
    my_skeleton = pick_index(skeletons, myself)
    root_rows = jnp.sum(jnp.where(my_root_slot[:, None] == iota(RANK)[None, :] + 1, my_skeleton[:, None] + 1, 0), axis=0) - 1
    root_pick = (root_rows[:, None] == iota(ROWS)[None, :]).astype(F32)
    root = jnp.dot(root_pick, root, precision=lax.Precision.HIGHEST) + root_arrivals

    half = RANK // 2
    kept = jnp.where(side == 0, root[:half], root[half:])
    kept = kept + shifted(jnp.where(side == 0, root[half:], root[:half]), cores)
    kept, owners, targets, incoming = lax.optimization_barrier((kept, owners, targets, incoming))
    kept = total_over_ring(kept, along_z)
    kept, yours = lax.optimization_barrier((kept, yours))
    kept = total_over_ring(kept, along_x)
    other = shifted(kept, cores)
    root = jnp.concatenate([jnp.where(side == 0, kept, other), jnp.where(side == 0, other, kept)], axis=0)

    hits = (owners == myself).astype(BF)
    before = (iota(LANES)[:, None] < iota(LANES)[None, :]).astype(BF)
    row = iota(leaf_total * groups)
    above = ((row[:, None] // groups == row[None, :] // groups) & (row[:, None] > row[None, :])).astype(BF)
    counts = jnp.dot(hits, jnp.ones((LANES, LANES), BF), preferred_element_type=F32).astype(BF)
    order = jnp.dot(hits, before, preferred_element_type=F32) + jnp.dot(above, counts, preferred_element_type=F32)
    placed = jnp.where(owners == myself, order.astype(jnp.int32), CAP).reshape(leaf_total, groups, LANES)
    slot_hits = placed[:, :, :, None] == iota(CAP)
    slot_rows = jnp.sum(jnp.where(slot_hits, targets.reshape(leaf_total, groups, LANES)[:, :, :, None] + 1, 0), axis=(1, 2)) - 1
    selector = (iota(ROWS)[:, None] == slot_rows.reshape(-1)[None, :]).astype(BF)
    full = full + jnp.dot(selector, incoming, preferred_element_type=F32)
    parent = full.astype(BF)

    pair_choice = pick_index(merge_select[0], jnp.right_shift(myself, 1)) - side * RANK
    pair_rows = jnp.sum(jnp.where(iota(RANK)[:, None] == pair_choice[None, :], my_skeleton[:, None] + 1, 0), axis=0) - 1
    pair_pick = (pair_rows[:, None] == iota(ROWS)[None, :]).astype(F32)
    pair_gone = pair_terms(front, myself, own, yours, pick_index(skeletons, cores(myself))[None])
    pair = jnp.dot(pair_pick, full - pair_gone, precision=lax.Precision.HIGHEST)
    pair = pair + shifted(pair, cores)
    return (parent[None], pair[None], root[None])


def solution(mesh):
    in_specs = (
        P("front", "hss", None),
        P("front", "hss", None),
        P("front", "hss", None),
        P("front", None, None),
        P("front", None),
        P("front", None, None),
        P("front", None, None),
    )
    out_specs = (P("front", "hss", None), P("front", "hss", None), P("front", None, None))
    return jax.shard_map(body, mesh=mesh, in_specs=in_specs, out_specs=out_specs, check_vma=False)
```

```python
import functools

import jax
import jax.numpy as jnp
from jax import lax
from jax.experimental import pallas as pl
from jax.experimental.pallas import tpu as pltpu
from jax.sharding import PartitionSpec as P

ROWS = 608
SAMPLES = 256
RANK = 128
CHILD = 512
CAP = 64
BF = jnp.bfloat16
F32 = jnp.float32
LANES = 128
SUBLANES = 16
WINDOW = 768
PLACES = (0, 96, 64, 160)
RING = 4
TURNS = (0, 1, 3, 2)
AHEAD = 2
VMEM = 42 << 20


def pick_index(table, position):
    return lax.dynamic_index_in_dim(table, position, 0, keepdims=False)


def iota(n):
    return jnp.arange(n, dtype=jnp.int32)


def shifted(x, move):
    return lax.ppermute(x, "hss", [(i, move(i)) for i in range(lax.axis_size("hss"))])


def cores(i):
    return i ^ 1


def along_z(turn):
    return lambda i: i ^ 2 * TURNS[turn]


def along_x(turn):
    return lambda i: i ^ 8 * TURNS[turn]


def first(turn):
    return lambda i: along_x(turn)(i) if i % 2 else along_z(turn)(i)


def second(turn):
    return lambda i: along_z(turn)(i) if i % 2 else along_x(turn)(i)


def total_over_ring(x, along):
    near, far, opposite = [shifted(x, along(turn)) for turn in (1, 2, 3)]
    return (x + near) + (far + opposite)


def fate_kernel(me_ref, select_ref, skeleton_ref, slots_ref, keep_ref):
    me = me_ref[0]
    row = lax.broadcasted_iota(jnp.int32, (SUBLANES, RANK), 0)
    once = jnp.where(row == 0, 1.0, 0.0)
    carried = [jnp.where(row == 1, lax.broadcasted_iota(jnp.int32, (SUBLANES, RANK), 1) + 1, 0).astype(F32)]
    place = lax.broadcasted_iota(jnp.int32, (2 * RANK, RANK), 0)
    at = select_ref.shape[0]
    while at > 0:
        at -= len(carried)
        below = []
        for node, values in enumerate(carried):
            hit = jnp.where(place == select_ref[at + node : at + node + 1, :], 1.0, 0.0).astype(BF)
            spread = lax.dot_general((values + once).astype(BF), hit, (((1,), (1,)), ((), ())), preferred_element_type=F32)
            below += [spread[:, :RANK], spread[:, RANK:]]
        carried = below
    gone = []
    for leaf, values in enumerate(carried):
        slots_ref[leaf : leaf + 1, :] = values[1:2, :].astype(jnp.int32)
        apart = jnp.bitwise_xor(me, leaf)
        level = sum([jnp.where(apart >= (2 << h), 1, 0) for h in range(4)])
        names = skeleton_ref[leaf : leaf + 1, :]
        gone.append(jnp.where(values[0:1, :].astype(jnp.int32) >= level, names, -WINDOW))
    gone = jnp.concatenate(gone + [gone[0]] * (RANK - len(gone)), axis=0).T
    lane = lax.broadcasted_iota(jnp.int32, (RANK, WINDOW), 1)
    for leaf in range(len(carried)):
        named = jnp.where(lane - PLACES[leaf % 4] == gone[:, leaf : leaf + 1], 1.0, 0.0)
        keep = 1.0 - jnp.max(named, axis=0, keepdims=True)
        keep_ref[leaf : leaf + 1, :] = keep * jnp.where(me == leaf, 0.0, 1.0)


def fates(me, selections, skeletons):
    leaves = skeletons.shape[0]
    return pl.pallas_call(
        fate_kernel,
        in_specs=[pl.BlockSpec(memory_space=pltpu.SMEM), pl.BlockSpec(), pl.BlockSpec()],
        out_shape=[jax.ShapeDtypeStruct((leaves, RANK), jnp.int32), jax.ShapeDtypeStruct((leaves, WINDOW), F32)],
        compiler_params=pltpu.CompilerParams(vmem_limit_bytes=VMEM),
        cost_estimate=pl.CostEstimate(flops=leaves << 20, bytes_accessed=leaves << 12, transcendentals=0),
    )(me[None], selections, skeletons)


def window_tile(leaf):
    return 19 * leaf // 4 - jnp.where(leaf % 4 == 3, 1, 0)


def window_place(leaf):
    kind = leaf % 4
    return jnp.where(kind == 0, PLACES[0], jnp.where(kind == 1, PLACES[1], jnp.where(kind == 2, PLACES[2], PLACES[3])))


def leaf_of(me, whose, step, j):
    by_first = 2 * TURNS[j] + 8 * TURNS[step]
    by_second = 8 * TURNS[j] + 2 * TURNS[step]
    side = jnp.bitwise_and(me, 1)
    moved = jnp.where(side == whose, by_first, by_second)
    return jnp.bitwise_xor(jnp.bitwise_xor(me, whose), moved)


def product_kernel(units, plain, masked, added, me_ref, front, keep_ref, *refs):
    blocks, refs = refs[: units[-1][0] + 1], refs[units[-1][0] + 1 :]
    out_ref, left_buf, right_buf, sems = refs[-4:]
    leaves = [leaf_of(me_ref[0], *unit[2:]) for unit in units]

    def copies(u):
        block, row = units[u][:2]
        slot, half = u // 2 % (AHEAD + 1), u % 2
        columns = pl.ds(pl.multiple_of(window_tile(leaves[u]) * LANES, LANES), WINDOW)
        rows = pl.ds(pl.multiple_of(half * WINDOW + window_place(leaves[u]), 32), ROWS)
        return (
            pltpu.make_async_copy(
                front.at[:, columns], left_buf.at[slot, :, pl.ds(half * WINDOW, WINDOW)], sems.at[u, 0]
            ),
            pltpu.make_async_copy(blocks[block].at[row], right_buf.at[slot, rows, :], sems.at[u, 1]),
        )

    def begin(slot):
        for u in (2 * slot, 2 * slot + 1):
            edge, into = (u % 2) * WINDOW, slot % (AHEAD + 1)
            right_buf[into, edge : edge + PLACES[-1], :] = jnp.zeros((PLACES[-1], SAMPLES), BF)
            right_buf[into, edge + ROWS : edge + WINDOW, :] = jnp.zeros((WINDOW - ROWS, SAMPLES), BF)
            for copy in copies(u):
                copy.start()

    slots = len(units) // 2
    for slot in range(min(AHEAD, slots)):
        begin(slot)
    for slot in range(slots):
        for u in (2 * slot, 2 * slot + 1):
            for copy in copies(u):
                copy.wait()
        if slot + AHEAD < slots:
            begin(slot + AHEAD)
        at = 0
        for kind in [0] * plain + [1] * masked:
            left = left_buf[slot % (AHEAD + 1)]
            if kind:
                keep = [keep_ref[pl.ds(leaves[2 * slot + half], 1), :].astype(BF) for half in range(2)]
                left = left * jnp.concatenate(keep, axis=1)
            value = jnp.dot(left, right_buf[slot % (AHEAD + 1)], preferred_element_type=F32)
            rows = pl.ds(at, ROWS)
            if slot:
                out_ref[rows, :] += value
            elif added:
                out_ref[rows, :] = refs[0][rows, :] + value
            else:
                out_ref[rows, :] = value
            at += ROWS


def products(front, me, keep, parts, start=None, plain=True, masked=True):
    blocks = [part[0] for part in parts]
    units = [(i, row, part[1], part[2], part[3] + row) for i, part in enumerate(parts) for row in range(2)]
    out = jax.ShapeDtypeStruct(((plain + masked) * ROWS, SAMPLES), F32)
    anywhere = pl.BlockSpec(memory_space=pl.ANY)
    whole = lambda array: pl.BlockSpec(array.shape, lambda i, s: (0, 0))
    return pl.pallas_call(
        functools.partial(product_kernel, units, plain, masked, start is not None),
        grid_spec=pltpu.PrefetchScalarGridSpec(
            num_scalar_prefetch=1,
            grid=(1,),
            in_specs=[anywhere, whole(keep)] + [anywhere] * len(blocks) + ([] if start is None else [whole(start)]),
            out_specs=whole(out),
            scratch_shapes=[
                pltpu.VMEM((AHEAD + 1, ROWS, 2 * WINDOW), BF),
                pltpu.VMEM((AHEAD + 1, 2 * WINDOW, SAMPLES), BF),
                pltpu.SemaphoreType.DMA((len(units), 2)),
            ],
        ),
        out_shape=out,
        input_output_aliases={} if start is None else {3 + len(blocks): 0},
        compiler_params=pltpu.CompilerParams(vmem_limit_bytes=VMEM),
        cost_estimate=pl.CostEstimate(
            flops=len(units) * out.shape[0] * WINDOW * SAMPLES // 2,
            bytes_accessed=len(units) * ROWS * WINDOW // 2,
            transcendentals=0,
        ),
    )(me[None], front, keep, *blocks, *([] if start is None else [start]))


def pair_kernel(me_ref, front, mine_ref, yours_ref, names_ref, out_ref, left_buf, right_buf, sems):
    leaves = (me_ref[0], jnp.bitwise_xor(me_ref[0], 1))
    copies = [
        pltpu.make_async_copy(
            front.at[:, pl.ds(pl.multiple_of(window_tile(leaf) * LANES, LANES), WINDOW)],
            left_buf.at[:, pl.ds(half * WINDOW, WINDOW)],
            sems.at[half],
        )
        for half, leaf in enumerate(leaves)
    ]
    for copy in copies:
        copy.start()
    named = jnp.where(lax.broadcasted_iota(jnp.int32, (ROWS, RANK), 0) == names_ref[...], 1.0, 0.0).astype(BF)
    count = jnp.dot(named, jnp.ones((RANK, SAMPLES), BF), preferred_element_type=F32).astype(BF)
    right_buf[...] = jnp.zeros_like(right_buf)
    for half, leaf in enumerate(leaves):
        at = pl.ds(pl.multiple_of(half * WINDOW + window_place(leaf), 32), ROWS)
        right_buf[at, :] = yours_ref[...] * count if half else mine_ref[...]
    for copy in copies:
        copy.wait()
    out_ref[...] = jnp.dot(left_buf[...], right_buf[...], preferred_element_type=F32)


def pair_terms(front, me, mine, yours, names):
    whole = lambda array: pl.BlockSpec(array.shape, lambda i, s: (0, 0))
    return pl.pallas_call(
        pair_kernel,
        grid_spec=pltpu.PrefetchScalarGridSpec(
            num_scalar_prefetch=1,
            grid=(1,),
            in_specs=[pl.BlockSpec(memory_space=pl.ANY), whole(mine), whole(yours), whole(names)],
            out_specs=pl.BlockSpec((ROWS, SAMPLES), lambda i, s: (0, 0)),
            scratch_shapes=[
                pltpu.VMEM((ROWS, 2 * WINDOW), BF),
                pltpu.VMEM((2 * WINDOW, SAMPLES), BF),
                pltpu.SemaphoreType.DMA((2,)),
            ],
        ),
        out_shape=jax.ShapeDtypeStruct((ROWS, SAMPLES), F32),
        compiler_params=pltpu.CompilerParams(vmem_limit_bytes=VMEM),
        cost_estimate=pl.CostEstimate(flops=4 * ROWS * WINDOW * SAMPLES, bytes_accessed=4 * ROWS * WINDOW, transcendentals=0),
    )(me[None], front, mine, yours, names)


def body(front_rows, samples, child_rows, child_owner, child_local, leaf_skeleton, merge_select):
    leaf_total = lax.axis_size("hss")
    myself = lax.axis_index("hss")
    side = jnp.bitwise_and(myself, 1)
    front = front_rows[0]
    skeletons = leaf_skeleton[0]

    own = samples[0]
    turned = [own] + [shifted(own, first(turn)) for turn in (1, 2, 3)]
    root_slot, keep = fates(myself, merge_select[0], skeletons)

    groups = CHILD // LANES
    owners = lax.reshape(child_owner, (leaf_total * groups, LANES))
    targets = lax.reshape(child_local, (leaf_total * groups, LANES))
    my_owners = lax.dynamic_slice_in_dim(owners, myself * groups, groups, 0).reshape(-1)
    my_targets = my_owners * ROWS + lax.dynamic_slice_in_dim(targets, myself * groups, groups, 0).reshape(-1)
    earlier = iota(CHILD)[:, None] < iota(CHILD)[None, :]
    my_slots = jnp.sum(((my_owners[:, None] == my_owners[None, :]) & earlier).astype(jnp.int32), axis=0)
    destination = my_owners * CAP + my_slots
    send_select = (iota(leaf_total * CAP)[:, None] == destination[None, :]).astype(BF)
    outgoing = jnp.dot(send_select, child_rows[0], preferred_element_type=F32).astype(BF)
    all_rows = iota(leaf_total)[:, None] * ROWS + skeletons + 1
    root_ids = jnp.sum(
        jnp.where(root_slot[:, :, None] == iota(RANK)[None, None, :] + 1, all_rows[:, :, None], 0), axis=(0, 1)
    ) - 1
    root_hits = (root_ids[:, None] == my_targets[None, :]).astype(BF)
    root_arrivals = jnp.dot(root_hits, child_rows[0], preferred_element_type=F32)

    turned, keep, outgoing = lax.optimization_barrier((turned, keep, outgoing))
    lines = [jnp.stack(turned[:2]), jnp.stack(turned[2:])]
    far_a = shifted(lines[0], second(2))
    near_b = shifted(lines[1], second(1))

    def both(block, step, turn):
        return [(block, 0, step, turn), (shifted(block, cores), 1, step, turn)]

    parts = both(lines[0], 0, 0) + both(lines[1], 0, 2)
    total = products(front, myself, keep, parts)
    yours = parts[1][0][0]
    far_a, near_b, lines, total, root_arrivals = lax.optimization_barrier((far_a, near_b, lines, total, root_arrivals))
    opposite = [shifted(far_a, second(1)), shifted(near_b, second(2))]
    near_a = shifted(lines[0], second(1))
    far_b = shifted(lines[1], second(2))
    total = products(front, myself, keep, both(far_a, 2, 0) + both(near_b, 1, 2), total)
    outgoing, total = lax.optimization_barrier((outgoing, total))
    near_a, far_b, opposite, total = lax.optimization_barrier((near_a, far_b, opposite, total))
    incoming = lax.all_to_all(
        outgoing.reshape(leaf_total, CAP, SAMPLES), "hss", split_axis=0, concat_axis=0, tiled=True
    ).reshape(leaf_total * CAP, SAMPLES)
    total = products(front, myself, keep, both(near_a, 1, 0) + both(far_b, 2, 2), total)
    total = products(front, myself, keep, both(opposite[0], 3, 0) + both(opposite[1], 3, 2), total)
    total, incoming = lax.optimization_barrier((total, incoming))
    full, root = total[:ROWS], total[ROWS:]
    my_root_slot = pick_index(root_slot, myself)
    my_skeleton = pick_index(skeletons, myself)
    root_rows = jnp.sum(jnp.where(my_root_slot[:, None] == iota(RANK)[None, :] + 1, my_skeleton[:, None] + 1, 0), axis=0) - 1
    root_pick = (root_rows[:, None] == iota(ROWS)[None, :]).astype(F32)
    root = jnp.dot(root_pick, root, precision=lax.Precision.HIGHEST) + root_arrivals

    half = RANK // 2
    kept = jnp.where(side == 0, root[:half], root[half:])
    kept = kept + shifted(jnp.where(side == 0, root[half:], root[:half]), cores)
    kept, owners, targets, incoming = lax.optimization_barrier((kept, owners, targets, incoming))
    kept = total_over_ring(kept, along_z)
    kept, yours = lax.optimization_barrier((kept, yours))
    kept = total_over_ring(kept, along_x)
    other = shifted(kept, cores)
    root = jnp.concatenate([jnp.where(side == 0, kept, other), jnp.where(side == 0, other, kept)], axis=0)

    hits = (owners == myself).astype(BF)
    before = (iota(LANES)[:, None] < iota(LANES)[None, :]).astype(BF)
    row = iota(leaf_total * groups)
    above = ((row[:, None] // groups == row[None, :] // groups) & (row[:, None] > row[None, :])).astype(BF)
    counts = jnp.dot(hits, jnp.ones((LANES, LANES), BF), preferred_element_type=F32).astype(BF)
    order = jnp.dot(hits, before, preferred_element_type=F32) + jnp.dot(above, counts, preferred_element_type=F32)
    placed = jnp.where(owners == myself, order.astype(jnp.int32), CAP).reshape(leaf_total, groups, LANES)
    slot_hits = placed[:, :, :, None] == iota(CAP)
    slot_rows = jnp.sum(jnp.where(slot_hits, targets.reshape(leaf_total, groups, LANES)[:, :, :, None] + 1, 0), axis=(1, 2)) - 1
    selector = (iota(ROWS)[:, None] == slot_rows.reshape(-1)[None, :]).astype(BF)
    full = full + jnp.dot(selector, incoming, preferred_element_type=F32)
    parent = full.astype(BF)

    pair_choice = pick_index(merge_select[0], jnp.right_shift(myself, 1)) - side * RANK
    pair_rows = jnp.sum(jnp.where(iota(RANK)[:, None] == pair_choice[None, :], my_skeleton[:, None] + 1, 0), axis=0) - 1
    pair_pick = (pair_rows[:, None] == iota(ROWS)[None, :]).astype(F32)
    pair_gone = pair_terms(front, myself, own, yours, pick_index(skeletons, cores(myself))[None])
    pair = jnp.dot(pair_pick, full - pair_gone, precision=lax.Precision.HIGHEST)
    pair = pair + shifted(pair, cores)
    return (parent[None], pair[None], root[None])


def solution(mesh):
    in_specs = (
        P("front", "hss", None),
        P("front", "hss", None),
        P("front", "hss", None),
        P("front", None, None),
        P("front", None),
        P("front", None, None),
        P("front", None, None),
    )
    out_specs = (P("front", "hss", None), P("front", "hss", None), P("front", None, None))
    return jax.shard_map(body, mesh=mesh, in_specs=in_specs, out_specs=out_specs, check_vma=False)
```
